32 devices in a mesh: head: 2 (over x), seq: 16 (over z, y, core).
Axes of the slice: x: 2, y: 2, z: 4, core: 2. Of those that a mesh axis runs over, the one named last changes fastest.
Arguments:
- tokens: bfloat16 [12288, 3200], P('seq'), may hold values from -6 to 6
- ln_gain: float32 [3200], replicated, may hold values from 0.5 to 2
- w_query: bfloat16 [3200, 2048], P('seq', 'head')
- w_key: bfloat16 [3200, 2048], P('seq', 'head')
- w_value: bfloat16 [3200, 2048], P('seq', 'head'), may hold values from -0.109375 to 0.109375
- q_gain: float32 [2048], P('head'), may hold values from 0.5 to 8
- k_gain: float32 [2048], P('head'), may hold values from 0.5 to 8
- seg_ids: int32 [12288], P('seq'), may hold values from 0 to 22, never falling along the last dimension, each value on 1 to 1025 neighbouring positions
Outputs:
- attended: bfloat16 [12288, 2048], P('seq', 'head')
The draws below stay inside these ranges and needn't reach their ends.
Inputs may be any that keep to these rules, and one draw needn't show every extreme that they name: `seg_ids`: ids never fall along the tokens; each id covers 1 to 1025 consecutive tokens and one covers exactly 1025.
All inputs are finite; a program needn't handle non-finite values.
Results may differ from the reference program's by a relative error of at most 0.0055.
The reference program's roundings to bfloat16 on the way (of `normed`, `q_hat` and `weights`) count: a program that leaves them out, or rounds other values in their place, can miss the bound.
Values may be sent and summed in bfloat16 or wider, within the bound.
A program may use at most 192 MiB of HBM per device.

```python
import math
import jax
import jax.numpy as jnp
import numpy as np
from jax import lax

D = 3200
HEADS = 16
HEAD_DIM = 128
MOST = 1025
TOK_DEV = 768
TOKENS = 12288
CHANNELS = 2048
SEGS = 23
N_SEQ = 16


def projection_draw(key, salt):
    own_key = jax.random.fold_in(key, salt)
    columns = HEADS * HEAD_DIM
    base = jnp.clip(jax.random.normal(own_key, (D, columns), jnp.float32), -6.0, 6.0)
    head_of = (jnp.arange(columns) // HEAD_DIM).astype(jnp.float32)
    scaled = 3.0 ** (head_of / max(HEADS - 1, 1)) / math.sqrt(D)
    return base * scaled[None, :]


def gain_draw(key, salt):
    own_key = jax.random.fold_in(key, salt)
    columns = HEADS * HEAD_DIM
    logs = jax.random.uniform(own_key, (columns,), jnp.float32, math.log(0.5), math.log(2.5))
    return jnp.exp(logs)


def draw_w_query(key, part):
    return projection_draw(key, 11).astype(jnp.bfloat16)


def draw_w_key(key, part):
    return projection_draw(key, 12).astype(jnp.bfloat16)


def draw_q_gain(key, part):
    return gain_draw(key, 21)


def draw_k_gain(key, part):
    return gain_draw(key, 22)


def steps_of(rng, extent, split, smallest, largest):
    def one(dim, parts):
        draws = jax.random.uniform(jax.random.fold_in(jax.random.fold_in(rng, 6), dim), (parts,), jnp.float32, smallest / len(split), largest / len(split))
        return jnp.repeat(jnp.exp(draws), extent[dim] // parts).reshape((-1,) + (1,) * (len(extent) - dim - 1))

    level = one(*split[0])
    for cut in split[1:]:
        level = level * one(*cut)
    return level


def length_profile(count, total, bound, skew):
    loads = [(1 << 20) // math.isqrt(standing ** skew) + 1 for standing in range(2, count + 1)]
    surplus, counts = total - bound - (count - 1), [1] * (count - 1)
    while surplus > 0:
        candidates = [i for i in range(count - 1) if counts[i] < bound]
        pool, budget = sum([loads[i] for i in candidates]), surplus
        for i in candidates:
            more = min(bound - counts[i], max(1, budget * loads[i] // pool), surplus)
            counts[i] = counts[i] + more
            surplus = surplus - more
    return np.array([bound] + counts)


def ragged_sizes(key, count, total, limit, skew):
    if count == 2:
        one = jax.random.randint(key, (), max(1, total - limit), min(limit, total - 1) + 1)
        return jnp.stack([one, total - one])
    sizes = jnp.asarray(length_profile(count, total, limit, skew), jnp.int32)
    couples = (count - 1) // 2
    donor, receiver = sizes[1:1 + 2 * couples:2], sizes[2:2 + 2 * couples:2]
    room = jnp.minimum(donor - 1, limit - receiver)
    moved = jax.random.randint(jax.random.fold_in(key, 1), (couples,), 0, 1 << 20) % (room + 1)
    sizes = sizes.at[1:1 + 2 * couples:2].set(donor - moved).at[2:2 + 2 * couples:2].set(receiver + moved)
    return sizes[jax.random.permutation(jax.random.fold_in(key, 2), count)]


def centred(stream_key, extent, scale, bound, cuts=(), kind=jnp.bfloat16):
    loudness = steps_of(stream_key, extent, cuts, -0.22, 0.18) if cuts else 1.0
    array = jax.random.normal(stream_key, extent, jnp.float32) * scale * loudness
    return jnp.minimum(jnp.maximum(array, -bound), bound).astype(kind)


def setup_inputs(seed: int = 0) -> dict:
    key_of = jax.random.split(jax.random.key(seed), 9)
    tokens = centred(key_of[0], (TOKENS, D), 1.0, 6.0, ((0, 16),))
    ln_gain = jnp.clip(jnp.exp(jax.random.uniform(key_of[1], (D,), jnp.float32, math.log(0.5), math.log(2.0))), 0.5, 2.0)
    w_query = draw_w_query(jax.random.fold_in(key_of[8], 71), 0)
    w_key = draw_w_key(jax.random.fold_in(key_of[8], 71), 0)
    w_value = centred(key_of[4], (D, CHANNELS), D ** -0.5, 0.109375, ((0, 16), (1, 2)))
    q_gain = draw_q_gain(jax.random.fold_in(key_of[8], 71), 0)
    k_gain = draw_k_gain(jax.random.fold_in(key_of[8], 71), 0)
    seg_ids = jnp.searchsorted(jnp.cumsum(ragged_sizes(key_of[7], SEGS, TOKENS, MOST, 2)), jnp.arange(TOKENS), side="right").astype(jnp.int32)
    return dict(tokens=tokens, ln_gain=ln_gain, w_query=w_query, w_key=w_key, w_value=w_value, q_gain=q_gain, k_gain=k_gain, seg_ids=seg_ids)


EPS = 1e-06

def rms_scale(values, gain, count):
    return values * lax.rsqrt(lax.optimization_barrier(jnp.sum(values * values, axis=1, keepdims=True)) / count + EPS) * gain

def reference(tokens, ln_gain, w_query, w_key, w_value, q_gain, k_gain, seg_ids):
    floats = tokens.astype(jnp.float32)
    normed = (floats * lax.rsqrt(lax.optimization_barrier(jnp.mean(floats * floats, axis=1, keepdims=True)) + EPS) * ln_gain).astype(jnp.bfloat16)
    channels = HEADS * HEAD_DIM
    queries = jnp.dot(normed, w_query, preferred_element_type=jnp.float32)
    key_part = jnp.dot(normed, w_key, preferred_element_type=jnp.float32)
    value_part = jnp.dot(normed, w_value, preferred_element_type=jnp.float32)
    q_hat = lax.optimization_barrier(rms_scale(queries, q_gain, channels).astype(jnp.bfloat16))
    k_hat = lax.optimization_barrier(rms_scale(key_part, k_gain, channels).astype(jnp.bfloat16))
    v_hat = lax.optimization_barrier(value_part.astype(jnp.bfloat16))
    margin = MOST - 1
    keys_padded = jnp.pad(k_hat, ((margin, margin), (0, 0)))
    values_padded = jnp.pad(v_hat, ((margin, margin), (0, 0)))
    marks = (seg_ids + 1).astype(jnp.int32)
    marks_padded = jnp.pad(marks, (margin, margin))
    span = TOK_DEV + 2 * margin
    scale = 1.0 / math.sqrt(HEAD_DIM)

    def one_block(index):
        start = (index * TOK_DEV).astype(jnp.int32)
        q_block = lax.dynamic_slice_in_dim(q_hat, start, TOK_DEV, 0).astype(jnp.float32)
        k_block = lax.dynamic_slice_in_dim(keys_padded, start, span, 0).astype(jnp.float32)
        v_block = lax.dynamic_slice_in_dim(values_padded, start, span, 0).astype(jnp.float32)
        own_marks = lax.dynamic_slice_in_dim(marks, start, TOK_DEV, 0)
        near_marks = lax.dynamic_slice_in_dim(marks_padded, start, span, 0)
        q_heads = q_block.reshape(TOK_DEV, HEADS, HEAD_DIM)
        k_heads = k_block.reshape(span, HEADS, HEAD_DIM)
        v_heads = v_block.reshape(span, HEADS, HEAD_DIM)
        scores = jnp.einsum('qhd,khd->hqk', q_heads, k_heads) * scale
        allowed = own_marks[:, None] == near_marks[None, :]
        scores = jnp.where(allowed[None, :, :], scores, -1e+30)
        highest = lax.optimization_barrier(jnp.max(scores, axis=2, keepdims=True))
        expo = jnp.exp(scores - highest)
        weights = expo / lax.optimization_barrier(jnp.sum(expo, axis=2, keepdims=True))
        weights = lax.optimization_barrier(weights.astype(jnp.bfloat16)).astype(jnp.float32)
        mixed = jnp.einsum('hqk,khd->qhd', weights, v_heads)
        return mixed.reshape(TOK_DEV, channels).astype(jnp.bfloat16)
    blocks = lax.map(one_block, jnp.arange(N_SEQ, dtype=jnp.int32))
    return blocks.reshape(TOKENS, channels)
```

```python
import functools
import math

import jax
import jax.numpy as jnp
from jax import lax
from jax.experimental import pallas as pl
from jax.experimental.pallas import tpu as pltpu
from jax.sharding import PartitionSpec as P

HEADS = 16
HEAD_DIM = 128
MOST = 1025
EPS = 1e-06
GROUP = 4
CHUNKS = 4
BLOCK = 256
MESH = pl.DeviceIdType.MESH
ANY = pl.BlockSpec(memory_space=pl.ANY)


def greet(partners):
    barrier = pltpu.get_barrier_semaphore()
    count = 0
    for device, there in partners:
        if there is None:
            pl.semaphore_signal(barrier, inc=1, device_id=device, device_id_type=MESH)
            count = count + 1
        else:

            @pl.when(there)
            def _(device=device):
                pl.semaphore_signal(barrier, inc=1, device_id=device, device_id_type=MESH)

            count = count + there.astype(jnp.int32)
    pl.semaphore_wait(barrier, count)


def remote(src, dst, send, recv, device):
    return pltpu.make_async_remote_copy(
        src_ref=src, dst_ref=dst, send_sem=send, recv_sem=recv,
        device_id=device, device_id_type=MESH,
    )


def gather_kernel(planes, n_ref, w_ref, x_out, w_out, own_sem, core_s, core_r, y_s, y_r, x_s, x_r,
                  cf_s, cf_r, a_s, a_r, up_s, up_r, down_s, down_r):
    h = lax.axis_index("head")
    s = lax.axis_index("seq")
    z, g = s // GROUP, s % GROUP
    y, c = g // 2, g % 2
    base = z * GROUP
    core_g = y * 2 + (1 - c)
    far_g = (1 - y) * 2 + c
    core_dev, y_dev, x_dev = (h, base + core_g), (h, base + far_g), (1 - h, s)
    up_dev = (h, jnp.minimum(s + GROUP, planes * GROUP - 1))
    down_dev = (h, jnp.maximum(s - GROUP, 0))
    has_up, has_down = z < planes - 1, z > 0
    group_dev = [(h, base + (g + d) % GROUP) for d in range(GROUP)]
    greet([(x_dev, None)] + [(group_dev[d], None) for d in range(1, GROUP)]
          + [(up_dev, has_up), (down_dev, has_down)])

    rows = n_ref.shape[0]
    half = rows // 2
    piece = half // CHUNKS

    def spread(d):
        return remote(w_ref.at[(g + d) % GROUP], w_out.at[s], a_s.at[d], a_r.at[d], group_dev[d])

    def climb(t, j):
        slot = (z - t) * GROUP + (g + GROUP - j) % GROUP
        src = w_ref.at[g] if (t, j) == (0, 0) else w_out.at[slot]
        return remote(src, w_out.at[slot], up_s.at[t * GROUP + j], up_r.at[t * GROUP + j], up_dev)

    def sink(t, j):
        slot = (z + t) * GROUP + (g + GROUP - j) % GROUP
        src = w_ref.at[g] if (t, j) == (0, 0) else w_out.at[slot]
        return remote(src, w_out.at[slot], down_s.at[t * GROUP + j], down_r.at[t * GROUP + j], down_dev)

    def any_slot(sem_s, sem_r, device):
        return remote(w_out.at[0], w_out.at[0], sem_s, sem_r, device)

    def token_rows(block, which, k):
        return x_out.at[block, pl.ds(pl.multiple_of(which * half + k * piece, 16), piece)]

    def over_y(k):
        first = pl.multiple_of(h * half + k * piece, 16)
        return remote(n_ref.at[pl.ds(first, piece)], token_rows(g, h, k), y_s.at[k], y_r.at[k], y_dev)

    def over_x(k):
        part = token_rows(far_g, h, k)
        return remote(part, part, x_s.at[k], x_r.at[k], x_dev)

    def over_core(k, from_x):
        part = token_rows(far_g, 1 - h if from_x else h, k)
        i = CHUNKS + k if from_x else k
        return remote(part, part, cf_s.at[i], cf_r.at[i], core_dev)

    own_w = pltpu.make_async_copy(w_ref.at[g], w_out.at[s], own_sem.at[0])
    own_x = pltpu.make_async_copy(n_ref, x_out.at[g], own_sem.at[1])
    block_core = remote(n_ref, x_out.at[g], core_s, core_r, core_dev)

    def send_z(t, j):
        @pl.when(jnp.logical_and(has_up, z - t >= 0))
        def _():
            climb(t, j).start()

        @pl.when(jnp.logical_and(has_down, z + t <= planes - 1))
        def _():
            sink(t, j).start()

    def take_z(t, j):
        i = t * GROUP + j

        @pl.when(z - 1 - t >= 0)
        def _():
            any_slot(up_s.at[i], up_r.at[i], down_dev).wait_recv()

        @pl.when(z + 1 + t <= planes - 1)
        def _():
            any_slot(down_s.at[i], down_r.at[i], up_dev).wait_recv()

        if t + 1 <= planes - 2:
            send_z(t + 1, j)

    send_z(0, 0)
    for d in (2, 1, 3):
        spread(d).start()
    for k in range(CHUNKS):
        over_y(k).start()
    block_core.start()
    own_w.start()
    own_x.start()
    for d in range(1, GROUP):
        spread(d).wait_recv()
        send_z(0, d)

    def take_y(k):
        over_y(k).wait_recv()
        over_x(k).start()
        over_core(k, False).start()

    def take_x(k):
        over_x(k).wait_recv()
        over_core(k, True).start()

    for k in range(CHUNKS):
        for j in range(k * GROUP // CHUNKS, (k + 1) * GROUP // CHUNKS):
            take_z(0, j)
        take_y(k)
        if k >= 1:
            take_x(k - 1)
        if k >= 2:
            take_z(1, k - 2)
    for j in range(CHUNKS - 2, GROUP):
        take_z(1, j)
    take_x(CHUNKS - 1)
    for t in range(2, planes - 1):
        for j in range(GROUP):
            take_z(t, j)

    own_w.wait()
    own_x.wait()
    block_core.wait()
    for k in range(CHUNKS):
        over_y(k).wait_send()
        over_x(k).wait_send()
        over_core(k, False).wait()
        over_core(k, True).wait()
    for d in range(1, GROUP):
        spread(d).wait_send()
    for t in range(planes - 1):
        for j in range(GROUP):

            @pl.when(jnp.logical_and(has_up, z - t >= 0))
            def _():
                climb(t, j).wait_send()

            @pl.when(jnp.logical_and(has_down, z + t <= planes - 1))
            def _():
                sink(t, j).wait_send()


def gather_plane(planes, normed, wcat):
    rows, width = normed.shape
    _, w_rows, w_cols = wcat.shape
    dma = pltpu.SemaphoreType.DMA
    hops = (planes - 1) * GROUP
    return pl.pallas_call(
        functools.partial(gather_kernel, planes),
        out_shape=(
            jax.ShapeDtypeStruct((GROUP, rows, width), normed.dtype),
            jax.ShapeDtypeStruct((planes * GROUP, w_rows, w_cols), wcat.dtype),
        ),
        in_specs=[ANY, ANY],
        out_specs=(ANY, ANY),
        scratch_shapes=[
            dma((2,)), dma, dma, dma((CHUNKS,)), dma((CHUNKS,)), dma((CHUNKS,)), dma((CHUNKS,)),
            dma((2 * CHUNKS,)), dma((2 * CHUNKS,)), dma((GROUP,)), dma((GROUP,)),
            dma((hops,)), dma((hops,)), dma((hops,)), dma((hops,)),
        ],
        compiler_params=pltpu.CompilerParams(collective_id=0, has_side_effects=True),
        name="gather_plane",
    )(normed, wcat)


def sums_kernel(part_ref, out_ref, slots, send, recv):
    h = lax.axis_index("head")
    s = lax.axis_index("seq")
    g = s % GROUP
    base = s - g
    others = []
    for dh in range(2):
        for d in range(GROUP):
            if (dh, d) != (0, 0):
                others.append((((h + dh) % 2, base + (g + d) % GROUP), dh * GROUP + d))
    greet([(device, None) for device, _ in others])
    mine = h * GROUP + g
    copies = []
    for device, i in others:
        copy = remote(part_ref, slots.at[mine], send.at[i], recv.at[i], device)
        copy.start()
        copies.append(copy)
    slots[mine] = part_ref[...]
    for copy in copies:
        copy.wait()
    total = slots[0]
    for i in range(1, 2 * GROUP):
        total = total + slots[i]
    out_ref[...] = total


def plane_sums(part):
    count = 2 * GROUP
    return pl.pallas_call(
        sums_kernel,
        out_shape=jax.ShapeDtypeStruct(part.shape, part.dtype),
        in_specs=[pl.BlockSpec(memory_space=pltpu.VMEM)],
        out_specs=pl.BlockSpec(memory_space=pltpu.VMEM),
        scratch_shapes=[
            pltpu.VMEM((count,) + part.shape, part.dtype),
            pltpu.SemaphoreType.DMA((count,)),
            pltpu.SemaphoreType.DMA((count,)),
        ],
        compiler_params=pltpu.CompilerParams(collective_id=1, has_side_effects=True),
        name="plane_sums",
    )(part)


def return_kernel(a_ref, o_ref, own, send, recv):
    h = lax.axis_index("head")
    s = lax.axis_index("seq")
    g = s % GROUP
    base = s - g
    width = a_ref.shape[2]
    greet([((h, base + (g + d) % GROUP), None) for d in range(1, GROUP)])
    columns = o_ref.at[:, pl.ds(pl.multiple_of(g * width, 128), width)]
    copies = []
    for d in (2, 3, 1):
        to = (g + d) % GROUP
        copy = remote(a_ref.at[to], columns, send.at[d], recv.at[d], (h, base + to))
        copy.start()
        copies.append(copy)
    here = pltpu.make_async_copy(a_ref.at[g], columns, own)
    here.start()
    here.wait()
    for copy in copies:
        copy.wait()


def return_tokens(attended):
    group, rows, width = attended.shape
    dma = pltpu.SemaphoreType.DMA
    return pl.pallas_call(
        return_kernel,
        out_shape=jax.ShapeDtypeStruct((rows, group * width), attended.dtype),
        in_specs=[ANY],
        out_specs=ANY,
        scratch_shapes=[dma, dma((GROUP,)), dma((GROUP,))],
        compiler_params=pltpu.CompilerParams(collective_id=2, has_side_effects=True),
        name="return_tokens",
    )(attended)


def attention_kernel(span_ref, q_ref, k_ref, v_ref, qm_ref, km_ref, o_ref, s_buf, m_buf, l_buf):
    block = pl.program_id(0)
    first, last = span_ref[0, block], span_ref[1, block]
    heads = q_ref.shape[1] // HEAD_DIM
    rate = math.log2(math.e) / math.sqrt(HEAD_DIM)
    own = jnp.broadcast_to(qm_ref[...], (BLOCK, BLOCK))
    for head in range(heads):
        cols = slice(head * HEAD_DIM, (head + 1) * HEAD_DIM)
        q = q_ref[:, cols]

        def lanes(x, op):
            out = x[:, :128]
            for i in range(1, BLOCK // 128):
                out = op(out, x[:, i * 128 : (i + 1) * 128])
            return out

        def score(b, highest):
            keys = k_ref[pl.ds(pl.multiple_of(b * BLOCK, BLOCK), BLOCK), cols]
            s = lax.dot_general(q, keys, (((1,), (1,)), ((), ())), preferred_element_type=jnp.float32)
            s = jnp.where(own == km_ref[b], s, -1e30)
            s_buf[b - first] = s
            return jnp.maximum(highest, lanes(s, jnp.maximum))

        highest = lax.fori_loop(first, last, score, jnp.full((BLOCK, 128), -1e30, jnp.float32))
        m = jnp.max(highest, axis=1, keepdims=True)

        def expo(b, total):
            e = jnp.exp2((s_buf[b - first] - m) * rate)
            s_buf[b - first] = e
            return total + lanes(e, jnp.add)

        total = lax.fori_loop(first, last, expo, jnp.zeros((BLOCK, 128), jnp.float32))
        share = 1.0 / jnp.sum(total, axis=1, keepdims=True)

        def mix(b, acc):
            w = (s_buf[b - first] * share).astype(jnp.bfloat16)
            values = v_ref[pl.ds(pl.multiple_of(b * BLOCK, BLOCK), BLOCK), cols]
            return acc + jnp.dot(w, values, preferred_element_type=jnp.float32)

        acc = lax.fori_loop(first, last, mix, jnp.zeros((BLOCK, HEAD_DIM), jnp.float32))
        o_ref[:, cols] = acc.astype(o_ref.dtype)


def attention(q_hat, near_k, near_v, own_marks, near_marks):
    rows, width = q_hat.shape
    near = near_k.shape[0]
    blocks, key_blocks = rows // BLOCK, near // BLOCK
    first_mark = own_marks[::BLOCK]
    last_mark = own_marks[BLOCK - 1 :: BLOCK]
    lowest = jnp.sum((near_marks[None, :] < first_mark[:, None]).astype(jnp.int32), axis=1)
    highest = jnp.sum((near_marks[None, :] <= last_mark[:, None]).astype(jnp.int32), axis=1)
    span = jnp.stack([lowest // BLOCK, (highest + BLOCK - 1) // BLOCK])
    most = min(key_blocks, (BLOCK + 2 * (MOST - 1)) // BLOCK + 1)
    pairs = rows * (BLOCK * 4) * (width // HEAD_DIM)
    return pl.pallas_call(
        attention_kernel,
        grid_spec=pltpu.PrefetchScalarGridSpec(
            num_scalar_prefetch=1,
            grid=(blocks,),
            in_specs=[
                pl.BlockSpec((BLOCK, width), lambda i, span: (i, 0)),
                pl.BlockSpec(memory_space=pltpu.VMEM),
                pl.BlockSpec(memory_space=pltpu.VMEM),
                pl.BlockSpec((BLOCK, 1), lambda i, span: (i, 0)),
                pl.BlockSpec(memory_space=pltpu.VMEM),
            ],
            out_specs=pl.BlockSpec((BLOCK, width), lambda i, span: (i, 0)),
            scratch_shapes=[
                pltpu.VMEM((most, BLOCK, BLOCK), jnp.float32),
                pltpu.VMEM((BLOCK, 128), jnp.float32),
                pltpu.VMEM((BLOCK, 128), jnp.float32),
            ],
        ),
        out_shape=jax.ShapeDtypeStruct((rows, width), jnp.bfloat16),
        compiler_params=pltpu.CompilerParams(vmem_limit_bytes=40 * 1024 * 1024),
        cost_estimate=pl.CostEstimate(
            flops=pairs * HEAD_DIM * 4, bytes_accessed=near * width * 4 + rows * width * 4,
            transcendentals=pairs),
        name="tile_attention",
    )(span, q_hat, near_k, near_v, own_marks[:, None], near_marks.reshape(key_blocks, 1, BLOCK))


def from_behind(shard, by):
    size = lax.axis_size("seq")
    pairs = [(i, i + by) for i in range(size) if 0 <= i + by < size]
    return lax.ppermute(shard, "seq", pairs)


def with_halo(shard, step):
    rows_here = shard.shape[0]
    left, right, need, distance = [], [], MOST - 1, 1
    while need > 0:
        take = min(need, rows_here)
        left.insert(0, from_behind(shard[rows_here - take :], distance * step))
        right.append(from_behind(shard[:take], -distance * step))
        need, distance = need - take, distance + 1
    return jnp.concatenate(left + [shard] + right, axis=0)


def on_device(grouped, tokens, ln_gain, w_query, w_key, w_value, q_gain, k_gain, seg_ids):
    heads_here = w_query.shape[1] // HEAD_DIM
    total_channels = HEADS * HEAD_DIM
    place = lax.axis_index("seq")
    seq = lax.axis_size("seq")
    margin = MOST - 1
    all_marks = lax.all_gather(seg_ids, "seq", axis=0, tiled=True)
    floats = tokens.astype(jnp.float32)
    normed = (
        floats * lax.rsqrt(jnp.mean(floats * floats, axis=1, keepdims=True) + EPS) * ln_gain
    ).astype(jnp.bfloat16)
    if grouped:
        share = w_query.shape[1] // GROUP
        step = GROUP
        member = place % GROUP
        wcat = jnp.concatenate(
            [w.reshape(w.shape[0], GROUP, share) for w in (w_key, w_value, w_query)], axis=2
        ).transpose(1, 0, 2)
        near_tokens, weights = gather_plane(seq // GROUP, normed, wcat)
        rows = GROUP * tokens.shape[0]
        near_tokens = near_tokens.reshape(rows, tokens.shape[1])
        weights = weights.reshape(tokens.shape[1], 3 * share)
        w_k, w_v, w_q = (weights[:, i * share : (i + 1) * share] for i in range(3))
        q_gain = lax.dynamic_slice_in_dim(q_gain, member * share, share)
        k_gain = lax.dynamic_slice_in_dim(k_gain, member * share, share)
    else:
        step = 1
        rows = tokens.shape[0]
        near_tokens = normed
        w_k, w_v, w_q = (
            lax.all_gather(w, "seq", axis=0, tiled=True) for w in (w_key, w_value, w_query)
        )

    def project(w):
        return jnp.dot(near_tokens, w, preferred_element_type=jnp.float32)

    def norm(part, gain):
        square = jnp.sum(part * part, axis=1)
        if grouped:
            square = plane_sums(square.reshape(rows // 128, 128)).reshape(rows)
        else:
            square = lax.psum(square, "head")
        return (part * lax.rsqrt(square[:, None] / total_channels + EPS) * gain).astype(jnp.bfloat16)

    near_v = with_halo(project(w_v).astype(jnp.bfloat16), step)
    near_k = with_halo(norm(project(w_k), k_gain), step)
    q_hat = norm(project(w_q), q_gain)

    low = jnp.full((margin,), -1, jnp.int32)
    high = jnp.full((margin,), jnp.iinfo(jnp.int32).max, jnp.int32)
    padded = jnp.concatenate([low, all_marks, high])
    first = place // step * rows
    near_marks = lax.dynamic_slice_in_dim(padded, first, rows + 2 * margin)
    own_marks = lax.slice_in_dim(near_marks, margin, margin + rows)
    attended = attention(q_hat, near_k, near_v, own_marks, near_marks)
    if grouped:
        attended = return_tokens(attended.reshape(GROUP, tokens.shape[0], attended.shape[1]))
    return attended


def solution(mesh):
    seq, heads = mesh.shape["seq"], mesh.shape["head"]
    grouped = heads == 2 and seq % GROUP == 0 and HEADS // heads % GROUP == 0
    return jax.shard_map(
        functools.partial(on_device, grouped),
        mesh=mesh,
        in_specs=(
            P("seq", None),
            P(),
            P("seq", "head"),
            P("seq", "head"),
            P("seq", "head"),
            P("head"),
            P("head"),
            P("seq"),
        ),
        out_specs=P("seq", "head"),
        check_vma=False,
    )
```

```python
import functools
import math

import jax
import jax.numpy as jnp
from jax import lax
from jax.experimental import pallas as pl
from jax.experimental.pallas import tpu as pltpu
from jax.sharding import PartitionSpec as P

HEADS = 16
HEAD_DIM = 128
MOST = 1025
EPS = 1e-06
GROUP = 4
CHUNKS = 4
BLOCK = 256
MESH = pl.DeviceIdType.MESH
ANY = pl.BlockSpec(memory_space=pl.ANY)


def greet(partners):
    barrier = pltpu.get_barrier_semaphore()
    count = 0
    for device, there in partners:
        if there is None:
            pl.semaphore_signal(barrier, inc=1, device_id=device, device_id_type=MESH)
            count = count + 1
        else:

            @pl.when(there)
            def _(device=device):
                pl.semaphore_signal(barrier, inc=1, device_id=device, device_id_type=MESH)

            count = count + there.astype(jnp.int32)
    pl.semaphore_wait(barrier, count)


def remote(src, dst, send, recv, device):
    return pltpu.make_async_remote_copy(
        src_ref=src, dst_ref=dst, send_sem=send, recv_sem=recv,
        device_id=device, device_id_type=MESH,
    )


def gather_kernel(planes, n_ref, w_ref, m_ref, x_out, w_out, m_out, own_sem, core_s, core_r, y_s, y_r, x_s, x_r,
                  cf_s, cf_r, a_s, a_r, up_s, up_r, down_s, down_r, mark_s, mark_r):
    h = lax.axis_index("head")
    s = lax.axis_index("seq")
    z, g = s // GROUP, s % GROUP
    y, c = g // 2, g % 2
    base = z * GROUP
    core_g = y * 2 + (1 - c)
    far_g = (1 - y) * 2 + c
    core_dev, y_dev, x_dev = (h, base + core_g), (h, base + far_g), (1 - h, s)
    up_dev = (h, jnp.minimum(s + GROUP, planes * GROUP - 1))
    down_dev = (h, jnp.maximum(s - GROUP, 0))
    has_up, has_down = z < planes - 1, z > 0
    member = [(y + d // 2) % 2 * 2 + (c + d % 2) % 2 for d in range(GROUP)]
    group_dev = [(h, base + m) for m in member]
    greet([(x_dev, None)] + [(group_dev[d], None) for d in range(1, GROUP)]
          + [(up_dev, has_up), (down_dev, has_down)])

    rows = n_ref.shape[0]
    half = rows // 2
    piece = half // CHUNKS

    def spread(d):
        return remote(w_ref.at[member[d]], w_out.at[s], a_s.at[d], a_r.at[d], group_dev[d])

    def climb(t, j):
        slot = (z - t) * GROUP + member[j]
        src = w_ref.at[g] if (t, j) == (0, 0) else w_out.at[slot]
        return remote(src, w_out.at[slot], up_s.at[t * GROUP + j], up_r.at[t * GROUP + j], up_dev)

    def sink(t, j):
        slot = (z + t) * GROUP + member[j]
        src = w_ref.at[g] if (t, j) == (0, 0) else w_out.at[slot]
        return remote(src, w_out.at[slot], down_s.at[t * GROUP + j], down_r.at[t * GROUP + j], down_dev)

    def any_slot(sem_s, sem_r, device):
        return remote(w_out.at[0], w_out.at[0], sem_s, sem_r, device)

    def token_rows(block, which, k):
        return x_out.at[block, pl.ds(pl.multiple_of(which * half + k * piece, 16), piece)]

    def over_y(k):
        first = pl.multiple_of(h * half + k * piece, 16)
        return remote(n_ref.at[pl.ds(first, piece)], token_rows(g, h, k), y_s.at[k], y_r.at[k], y_dev)

    def over_x(k):
        part = token_rows(far_g, h, k)
        return remote(part, part, x_s.at[k], x_r.at[k], x_dev)

    def over_core(k, from_x):
        part = token_rows(far_g, 1 - h if from_x else h, k)
        i = CHUNKS + k if from_x else k
        return remote(part, part, cf_s.at[i], cf_r.at[i], core_dev)

    own_w = pltpu.make_async_copy(w_ref.at[g], w_out.at[s], own_sem.at[0])
    own_x = pltpu.make_async_copy(n_ref, x_out.at[g], own_sem.at[1])
    block_core = remote(n_ref, x_out.at[g], core_s, core_r, core_dev)

    own_m = pltpu.make_async_copy(m_ref, m_out.at[1, g], own_sem.at[2])

    def spread_marks(d):
        return remote(m_ref, m_out.at[1, g], mark_s.at[d], mark_r.at[d], group_dev[d])

    marks_up = remote(m_out.at[1], m_out.at[0], mark_s.at[4], mark_r.at[4], up_dev)
    marks_down = remote(m_out.at[1], m_out.at[2], mark_s.at[5], mark_r.at[5], down_dev)

    def send_z(t, j):
        @pl.when(jnp.logical_and(has_up, z - t >= 0))
        def _():
            climb(t, j).start()

        @pl.when(jnp.logical_and(has_down, z + t <= planes - 1))
        def _():
            sink(t, j).start()

    def take_z(t, j):
        i = t * GROUP + j

        @pl.when(z - 1 - t >= 0)
        def _():
            any_slot(up_s.at[i], up_r.at[i], down_dev).wait_recv()

        @pl.when(z + 1 + t <= planes - 1)
        def _():
            any_slot(down_s.at[i], down_r.at[i], up_dev).wait_recv()

        if t + 1 <= planes - 2:
            send_z(t + 1, j)

    own_m.start()
    send_z(0, 0)
    for d in (1, 2, 3):
        spread(d).start()
        spread_marks(d).start()
    over_y(0).start()
    over_y(1).start()
    block_core.start()
    own_w.start()
    own_x.start()

    def take_y(k):
        over_y(k).wait_recv()
        over_x(k).start()
        over_core(k, False).start()
        if k + 2 < CHUNKS:
            over_y(k + 2).start()

    def take_x(k):
        over_x(k).wait_recv()
        over_core(k, True).start()

    def take_spread(d):
        spread(d).wait_recv()
        send_z(0, d)

    take_spread(1)
    take_z(0, 0)
    take_spread(2)
    take_spread(3)
    take_z(0, 1)
    own_m.wait()
    for d in range(1, GROUP):
        spread_marks(d).wait_recv()

    @pl.when(has_up)
    def _():
        marks_up.start()

    @pl.when(has_down)
    def _():
        marks_down.start()

    take_z(0, 2)
    take_y(0)
    hops = [(0, 3)] + [(t, j) for t in range(1, planes - 1) for j in range(GROUP)]
    moves = [(take_y, k) for k in range(1, CHUNKS)] + [(take_x, k) for k in range(CHUNKS)]
    moves.sort(key=lambda move: move[1] + (0.5 if move[0] is take_x else -0.5))
    done = 0
    for i, hop in enumerate(hops):
        take_z(*hop)
        until = min(len(moves), (i * len(moves) + len(hops) - 1) // max(len(hops) - 1, 1))
        for move, k in moves[done:until]:
            move(k)
        done = max(done, until)
    for move, k in moves[done:]:
        move(k)

    own_w.wait()
    own_x.wait()
    block_core.wait()
    for k in range(CHUNKS):
        over_y(k).wait_send()
        over_x(k).wait_send()
        over_core(k, False).wait()
        over_core(k, True).wait()
    for d in range(1, GROUP):
        spread(d).wait_send()
        spread_marks(d).wait_send()

    @pl.when(has_up)
    def _():
        marks_up.wait_send()
        marks_down.wait_recv()

    @pl.when(has_down)
    def _():
        marks_down.wait_send()
        marks_up.wait_recv()

    for t in range(planes - 1):
        for j in range(GROUP):

            @pl.when(jnp.logical_and(has_up, z - t >= 0))
            def _():
                climb(t, j).wait_send()

            @pl.when(jnp.logical_and(has_down, z + t <= planes - 1))
            def _():
                sink(t, j).wait_send()


def gather_plane(planes, normed, wcat, marks):
    rows, width = normed.shape
    _, w_rows, w_cols = wcat.shape
    dma = pltpu.SemaphoreType.DMA
    hops = (planes - 1) * GROUP
    return pl.pallas_call(
        functools.partial(gather_kernel, planes),
        out_shape=(
            jax.ShapeDtypeStruct((GROUP, rows, width), normed.dtype),
            jax.ShapeDtypeStruct((planes * GROUP, w_rows, w_cols), wcat.dtype),
            jax.ShapeDtypeStruct((3, GROUP) + marks.shape, marks.dtype),
        ),
        in_specs=[ANY, ANY, ANY],
        out_specs=(ANY, ANY, ANY),
        scratch_shapes=[
            dma((3,)), dma, dma, dma((CHUNKS,)), dma((CHUNKS,)), dma((CHUNKS,)), dma((CHUNKS,)),
            dma((2 * CHUNKS,)), dma((2 * CHUNKS,)), dma((GROUP,)), dma((GROUP,)),
            dma((hops,)), dma((hops,)), dma((hops,)), dma((hops,)), dma((6,)), dma((6,)),
        ],
        compiler_params=pltpu.CompilerParams(collective_id=0, has_side_effects=True),
        name="gather_plane",
    )(normed, wcat, marks)


def sums_kernel(part_ref, out_ref, slots, send, recv):
    h = lax.axis_index("head")
    s = lax.axis_index("seq")
    g = s % GROUP
    base = s - g
    others = []
    for dh in range(2):
        for d in range(GROUP):
            if (dh, d) != (0, 0):
                others.append((((h + dh) % 2, base + (g + d) % GROUP), dh * GROUP + d))
    greet([(device, None) for device, _ in others])
    mine = h * GROUP + g
    copies = []
    for device, i in others:
        copy = remote(part_ref, slots.at[mine], send.at[i], recv.at[i], device)
        copy.start()
        copies.append(copy)
    slots[mine] = part_ref[...]
    for copy in copies:
        copy.wait()
    total = slots[0]
    for i in range(1, 2 * GROUP):
        total = total + slots[i]
    out_ref[...] = total


def plane_sums(part):
    count = 2 * GROUP
    return pl.pallas_call(
        sums_kernel,
        out_shape=jax.ShapeDtypeStruct(part.shape, part.dtype),
        in_specs=[pl.BlockSpec(memory_space=pltpu.VMEM)],
        out_specs=pl.BlockSpec(memory_space=pltpu.VMEM),
        scratch_shapes=[
            pltpu.VMEM((count,) + part.shape, part.dtype),
            pltpu.SemaphoreType.DMA((count,)),
            pltpu.SemaphoreType.DMA((count,)),
        ],
        compiler_params=pltpu.CompilerParams(collective_id=1, has_side_effects=True),
        name="plane_sums",
    )(part)


def return_kernel(a_ref, o_ref, own, send, recv):
    h = lax.axis_index("head")
    s = lax.axis_index("seq")
    g = s % GROUP
    base = s - g
    width = a_ref.shape[2]
    greet([((h, base + (g + d) % GROUP), None) for d in range(1, GROUP)])
    columns = o_ref.at[:, pl.ds(pl.multiple_of(g * width, 128), width)]
    copies = []
    for d in (2, 3, 1):
        to = (g + d) % GROUP
        copy = remote(a_ref.at[to], columns, send.at[d], recv.at[d], (h, base + to))
        copy.start()
        copies.append(copy)
    here = pltpu.make_async_copy(a_ref.at[g], columns, own)
    here.start()
    here.wait()
    for copy in copies:
        copy.wait()


def return_tokens(attended):
    group, rows, width = attended.shape
    dma = pltpu.SemaphoreType.DMA
    return pl.pallas_call(
        return_kernel,
        out_shape=jax.ShapeDtypeStruct((rows, group * width), attended.dtype),
        in_specs=[ANY],
        out_specs=ANY,
        scratch_shapes=[dma, dma((GROUP,)), dma((GROUP,))],
        compiler_params=pltpu.CompilerParams(collective_id=2, has_side_effects=True),
        name="return_tokens",
    )(attended)


def lanes(x, op):
    out = x[:, :128]
    for i in range(1, BLOCK // 128):
        out = op(out, x[:, i * 128 : (i + 1) * 128])
    return out


def attention_kernel(span_ref, q_ref, k_ref, v_ref, qm_ref, km_ref, o_ref, s_buf):
    block = pl.program_id(0)
    first, last = span_ref[0, block], span_ref[1, block]
    heads = range(q_ref.shape[1] // HEAD_DIM)
    columns = [slice(head * HEAD_DIM, (head + 1) * HEAD_DIM) for head in heads]
    rate = math.log2(math.e) / math.sqrt(HEAD_DIM)
    own = jnp.broadcast_to(qm_ref[...], (BLOCK, BLOCK))

    def rows(b):
        return pl.ds(pl.multiple_of(b * BLOCK, BLOCK), BLOCK)

    def score(b, highest):
        allowed = own == km_ref[b]
        scores = [
            lax.dot_general(
                q_ref[:, columns[head]], k_ref[rows(b), columns[head]], (((1,), (1,)), ((), ())),
                preferred_element_type=jnp.float32)
            for head in heads
        ]
        out = []
        for head in heads:
            s = jnp.where(allowed, scores[head], -1e30)
            s_buf[head, b - first] = s
            out.append(jnp.maximum(highest[head], lanes(s, jnp.maximum)))
        return tuple(out)

    low = jnp.full((BLOCK, 128), -1e30, jnp.float32)
    highest = lax.fori_loop(first, last, score, tuple(low for _ in heads))
    tops = [jnp.max(x, axis=1, keepdims=True) for x in highest]

    def expo(b, totals):
        out = []
        for head in heads:
            e = jnp.exp2((s_buf[head, b - first] - tops[head]) * rate)
            s_buf[head, b - first] = e
            out.append(totals[head] + lanes(e, jnp.add))
        return tuple(out)

    zero = jnp.zeros((BLOCK, 128), jnp.float32)
    totals = lax.fori_loop(first, last, expo, tuple(zero for _ in heads))
    shares = [1.0 / jnp.sum(x, axis=1, keepdims=True) for x in totals]

    def mix(b, accs):
        out = []
        for head in heads:
            w = (s_buf[head, b - first] * shares[head]).astype(jnp.bfloat16)
            out.append(accs[head] + jnp.dot(
                w, v_ref[rows(b), columns[head]], preferred_element_type=jnp.float32))
        return tuple(out)

    accs = lax.fori_loop(first, last, mix, tuple(zero for _ in heads))
    for head in heads:
        o_ref[:, columns[head]] = accs[head].astype(o_ref.dtype)


def attention(q_hat, near_k, near_v, own_marks, near_marks):
    rows, width = q_hat.shape
    near = near_k.shape[0]
    blocks, key_blocks = rows // BLOCK, near // BLOCK
    first_mark = own_marks[::BLOCK]
    last_mark = own_marks[BLOCK - 1 :: BLOCK]
    lowest = jnp.sum((near_marks[None, :] < first_mark[:, None]).astype(jnp.int32), axis=1)
    highest = jnp.sum((near_marks[None, :] <= last_mark[:, None]).astype(jnp.int32), axis=1)
    span = jnp.stack([lowest // BLOCK, (highest + BLOCK - 1) // BLOCK])
    most = min(key_blocks, (BLOCK + 2 * (MOST - 1)) // BLOCK + 1)
    pairs = rows * (BLOCK * 4) * (width // HEAD_DIM)
    return pl.pallas_call(
        attention_kernel,
        grid_spec=pltpu.PrefetchScalarGridSpec(
            num_scalar_prefetch=1,
            grid=(blocks,),
            in_specs=[
                pl.BlockSpec((BLOCK, width), lambda i, span: (i, 0)),
                pl.BlockSpec(memory_space=pltpu.VMEM),
                pl.BlockSpec(memory_space=pltpu.VMEM),
                pl.BlockSpec((BLOCK, 1), lambda i, span: (i, 0)),
                pl.BlockSpec(memory_space=pltpu.VMEM),
            ],
            out_specs=pl.BlockSpec((BLOCK, width), lambda i, span: (i, 0)),
            scratch_shapes=[
                pltpu.VMEM((width // HEAD_DIM, most, BLOCK, BLOCK), jnp.float32),
            ],
        ),
        out_shape=jax.ShapeDtypeStruct((rows, width), jnp.bfloat16),
        compiler_params=pltpu.CompilerParams(vmem_limit_bytes=40 * 1024 * 1024),
        cost_estimate=pl.CostEstimate(
            flops=pairs * HEAD_DIM * 4, bytes_accessed=near * width * 4 + rows * width * 4,
            transcendentals=pairs),
        name="tile_attention",
    )(span, q_hat, near_k, near_v, own_marks[:, None], near_marks.reshape(key_blocks, 1, BLOCK))


def norm_kernel(t_ref, gain_ref, o_ref):
    floats = t_ref[...].astype(jnp.float32)
    square = jnp.mean(floats * floats, axis=1, keepdims=True)
    o_ref[...] = (floats * lax.rsqrt(square + EPS) * gain_ref[...]).astype(o_ref.dtype)


def norm_tokens(tokens, gain):
    rows, width = tokens.shape
    part = 128
    return pl.pallas_call(
        norm_kernel,
        grid=(rows // part,),
        in_specs=[
            pl.BlockSpec((part, width), lambda i: (i, 0)),
            pl.BlockSpec((1, width), lambda i: (0, 0)),
        ],
        out_specs=pl.BlockSpec((part, width), lambda i: (i, 0)),
        out_shape=jax.ShapeDtypeStruct((rows, width), jnp.bfloat16),
        compiler_params=pltpu.CompilerParams(vmem_limit_bytes=32 * 1024 * 1024),
        cost_estimate=pl.CostEstimate(
            flops=rows * width * 4, bytes_accessed=rows * width * 4, transcendentals=rows),
        name="norm_tokens",
    )(tokens, gain[None, :])


def from_behind(shard, by):
    size = lax.axis_size("seq")
    pairs = [(i, i + by) for i in range(size) if 0 <= i + by < size]
    return lax.ppermute(shard, "seq", pairs)


def with_halo(shard, step):
    rows_here = shard.shape[0]
    left, right, need, distance = [], [], MOST - 1, 1
    while need > 0:
        take = min(need, rows_here)
        left.insert(0, from_behind(shard[rows_here - take :], distance * step))
        right.append(from_behind(shard[:take], -distance * step))
        need, distance = need - take, distance + 1
    return jnp.concatenate(left + [shard] + right, axis=0)


def on_device(grouped, tokens, ln_gain, w_query, w_key, w_value, q_gain, k_gain, seg_ids):
    heads_here = w_query.shape[1] // HEAD_DIM
    total_channels = HEADS * HEAD_DIM
    place = lax.axis_index("seq")
    seq = lax.axis_size("seq")
    margin = MOST - 1
    normed = norm_tokens(tokens, ln_gain)
    low, high = -1, jnp.iinfo(jnp.int32).max
    if grouped:
        share = w_query.shape[1] // GROUP
        step = GROUP
        member = place % GROUP
        wcat = jnp.concatenate(
            [w.reshape(w.shape[0], GROUP, share) for w in (w_key, w_value, w_query)], axis=2
        ).transpose(1, 0, 2)
        near_tokens, weights, marks = gather_plane(
            seq // GROUP, normed, wcat, seg_ids.reshape(-1, 128)
        )
        plane = place // GROUP
        marks = marks.reshape(3, -1)
        own_marks = marks[1]
        left = jnp.where(plane > 0, marks[0, marks.shape[1] - margin :], low)
        right = jnp.where(plane < seq // GROUP - 1, marks[2, :margin], high)
        near_marks = jnp.concatenate([left, own_marks, right])
        rows = GROUP * tokens.shape[0]
        near_tokens = near_tokens.reshape(rows, tokens.shape[1])
        weights = weights.reshape(tokens.shape[1], 3 * share)
        q_gain = lax.dynamic_slice_in_dim(q_gain, member * share, share)
        k_gain = lax.dynamic_slice_in_dim(k_gain, member * share, share)
    else:
        step = 1
        rows = tokens.shape[0]
        near_tokens = normed
        share = w_query.shape[1]
        weights = jnp.concatenate([w_key, w_value, w_query], axis=1)
        weights = lax.all_gather(weights, "seq", axis=0, tiled=True)
        all_marks = lax.all_gather(seg_ids, "seq", axis=0, tiled=True)
        padded = jnp.concatenate(
            [jnp.full((margin,), low, jnp.int32), all_marks, jnp.full((margin,), high, jnp.int32)]
        )
        near_marks = lax.dynamic_slice_in_dim(padded, place * rows, rows + 2 * margin)
        own_marks = seg_ids

    def project(w):
        return jnp.dot(near_tokens, w, preferred_element_type=jnp.float32)

    def norm(part, gain):
        square = jnp.sum(part * part, axis=1)
        if grouped:
            square = plane_sums(square.reshape(rows // 128, 128)).reshape(rows)
        else:
            square = lax.psum(square, "head")
        return (part * lax.rsqrt(square[:, None] / total_channels + EPS) * gain).astype(jnp.bfloat16)

    both = project(weights[:, : 2 * share])
    near_v = with_halo(both[:, share:].astype(jnp.bfloat16), step)
    near_k = with_halo(norm(both[:, :share], k_gain), step)
    q_hat = norm(project(weights[:, 2 * share :]), q_gain)
    attended = attention(q_hat, near_k, near_v, own_marks, near_marks)
    if grouped:
        attended = return_tokens(attended.reshape(GROUP, tokens.shape[0], attended.shape[1]))
    return attended


def solution(mesh):
    seq, heads = mesh.shape["seq"], mesh.shape["head"]
    grouped = heads == 2 and seq % GROUP == 0 and HEADS // heads % GROUP == 0
    return jax.shard_map(
        functools.partial(on_device, grouped),
        mesh=mesh,
        in_specs=(
            P("seq", None),
            P(),
            P("seq", "head"),
            P("seq", "head"),
            P("seq", "head"),
            P("head"),
            P("head"),
            P("seq"),
        ),
        out_specs=P("seq", "head"),
        check_vma=False,
    )
```

```python
import functools
import math

import jax
import jax.numpy as jnp
from jax import lax
from jax.experimental import pallas as pl
from jax.experimental.pallas import tpu as pltpu
from jax.sharding import PartitionSpec as P

HEADS = 16
HEAD_DIM = 128
MOST = 1025
EPS = 1e-06
GROUP = 4
CHUNKS = 4
PIECES = 8
BLOCK = 256
MESH = pl.DeviceIdType.MESH
ANY = pl.BlockSpec(memory_space=pl.ANY)


def greet(partners):
    barrier = pltpu.get_barrier_semaphore()
    count = 0
    for device, there in partners:
        if there is None:
            pl.semaphore_signal(barrier, inc=1, device_id=device, device_id_type=MESH)
            count = count + 1
        else:

            @pl.when(there)
            def _(device=device):
                pl.semaphore_signal(barrier, inc=1, device_id=device, device_id_type=MESH)

            count = count + there.astype(jnp.int32)
    pl.semaphore_wait(barrier, count)


def remote(src, dst, send, recv, device):
    return pltpu.make_async_remote_copy(
        src_ref=src, dst_ref=dst, send_sem=send, recv_sem=recv,
        device_id=device, device_id_type=MESH,
    )


def gather_kernel(planes, n_ref, w_ref, m_ref, x_out, w_out, m_out, own_sem, core_s, core_r, y_s, y_r, x_s, x_r,
                  cf_s, cf_r, a_s, a_r, up_s, up_r, down_s, down_r, mark_s, mark_r):
    h = lax.axis_index("head")
    s = lax.axis_index("seq")
    z, g = s // GROUP, s % GROUP
    y, c = g // 2, g % 2
    base = z * GROUP
    core_g = y * 2 + (1 - c)
    far_g = (1 - y) * 2 + c
    core_dev, y_dev, x_dev = (h, base + core_g), (h, base + far_g), (1 - h, s)
    up_dev = (h, jnp.minimum(s + GROUP, planes * GROUP - 1))
    down_dev = (h, jnp.maximum(s - GROUP, 0))
    has_up, has_down = z < planes - 1, z > 0
    member = [(y + d // 2) % 2 * 2 + (c + d % 2) % 2 for d in range(GROUP)]
    group_dev = [(h, base + m) for m in member]
    greet([(x_dev, None)] + [(group_dev[d], None) for d in range(1, GROUP)]
          + [(up_dev, has_up), (down_dev, has_down)])

    rows = n_ref.shape[0]
    half = rows // 2
    piece = half // CHUNKS

    def spread(d):
        return remote(w_ref.at[member[d]], w_out.at[s], a_s.at[d], a_r.at[d], group_dev[d])

    def climb(t, j):
        slot = (z - t) * GROUP + member[j]
        src = w_ref.at[g] if (t, j) == (0, 0) else w_out.at[slot]
        return remote(src, w_out.at[slot], up_s.at[t * GROUP + j], up_r.at[t * GROUP + j], up_dev)

    def sink(t, j):
        slot = (z + t) * GROUP + member[j]
        src = w_ref.at[g] if (t, j) == (0, 0) else w_out.at[slot]
        return remote(src, w_out.at[slot], down_s.at[t * GROUP + j], down_r.at[t * GROUP + j], down_dev)

    def any_slot(sem_s, sem_r, device):
        return remote(w_out.at[0], w_out.at[0], sem_s, sem_r, device)

    def token_rows(block, which, k):
        return x_out.at[block, pl.ds(pl.multiple_of(which * half + k * piece, 16), piece)]

    def over_y(k):
        first = pl.multiple_of(h * half + k * piece, 16)
        return remote(n_ref.at[pl.ds(first, piece)], token_rows(g, h, k), y_s.at[k], y_r.at[k], y_dev)

    def over_x(k):
        part = token_rows(far_g, h, k)
        return remote(part, part, x_s.at[k], x_r.at[k], x_dev)

    def over_core(k, from_x):
        part = token_rows(far_g, 1 - h if from_x else h, k)
        i = CHUNKS + k if from_x else k
        return remote(part, part, cf_s.at[i], cf_r.at[i], core_dev)

    own_w = pltpu.make_async_copy(w_ref.at[g], w_out.at[s], own_sem.at[0])
    slab = rows // PIECES

    def own_x(i):
        part = pl.ds(i * slab, slab)
        return pltpu.make_async_copy(n_ref.at[part], x_out.at[g, part], own_sem.at[2 + i])

    def block_core(i):
        part = pl.ds(i * slab, slab)
        return remote(n_ref.at[part], x_out.at[g, part], core_s.at[i], core_r.at[i], core_dev)

    own_m = pltpu.make_async_copy(m_ref, m_out.at[1, g], own_sem.at[1])

    def spread_marks(d):
        return remote(m_ref, m_out.at[1, g], mark_s.at[d], mark_r.at[d], group_dev[d])

    marks_up = remote(m_out.at[1], m_out.at[0], mark_s.at[4], mark_r.at[4], up_dev)
    marks_down = remote(m_out.at[1], m_out.at[2], mark_s.at[5], mark_r.at[5], down_dev)

    def send_z(t, j):
        @pl.when(jnp.logical_and(has_up, z - t >= 0))
        def _():
            climb(t, j).start()

        @pl.when(jnp.logical_and(has_down, z + t <= planes - 1))
        def _():
            sink(t, j).start()

    def take_z(t, j):
        i = t * GROUP + j

        @pl.when(z - 1 - t >= 0)
        def _():
            any_slot(up_s.at[i], up_r.at[i], down_dev).wait_recv()

        @pl.when(z + 1 + t <= planes - 1)
        def _():
            any_slot(down_s.at[i], down_r.at[i], up_dev).wait_recv()

        if t + 1 <= planes - 2:
            send_z(t + 1, j)

    own_m.start()
    send_z(0, 0)
    for d in (1, 2, 3):
        spread(d).start()
        spread_marks(d).start()
    over_y(0).start()
    over_y(1).start()
    over_y(2).start()
    own_w.start()
    for i in range(PIECES):
        block_core(i).start()
        own_x(i).start()

    def take_y(k):
        over_y(k).wait_recv()
        over_x(k).start()
        over_core(k, False).start()
        if k + 3 < CHUNKS:
            over_y(k + 3).start()

    def take_x(k):
        over_x(k).wait_recv()
        over_core(k, True).start()

    def take_spread(d):
        spread(d).wait_recv()
        send_z(0, d)

    take_spread(1)
    take_z(0, 0)
    take_spread(2)
    take_spread(3)
    take_z(0, 1)
    own_m.wait()
    for d in range(1, GROUP):
        spread_marks(d).wait_recv()

    @pl.when(has_up)
    def _():
        marks_up.start()

    @pl.when(has_down)
    def _():
        marks_down.start()

    take_z(0, 2)
    take_y(0)
    hops = [(0, 3)] + [(t, j) for t in range(1, planes - 1) for j in range(GROUP)]
    moves = [(take_y, k) for k in range(1, CHUNKS)] + [(take_x, k) for k in range(CHUNKS)]
    moves.sort(key=lambda move: move[1] + (0.5 if move[0] is take_x else -0.5))
    done = 0
    for i, hop in enumerate(hops):
        take_z(*hop)
        until = min(len(moves), (i * len(moves) + len(hops) - 1) // max(len(hops) - 1, 1))
        for move, k in moves[done:until]:
            move(k)
        done = max(done, until)
    for move, k in moves[done:]:
        move(k)

    own_w.wait()
    for i in range(PIECES):
        own_x(i).wait()
        block_core(i).wait()
    for k in range(CHUNKS):
        over_y(k).wait_send()
        over_x(k).wait_send()
        over_core(k, False).wait()
        over_core(k, True).wait()
    for d in range(1, GROUP):
        spread(d).wait_send()
        spread_marks(d).wait_send()

    @pl.when(has_up)
    def _():
        marks_up.wait_send()
        marks_down.wait_recv()

    @pl.when(has_down)
    def _():
        marks_down.wait_send()
        marks_up.wait_recv()

    for t in range(planes - 1):
        for j in range(GROUP):

            @pl.when(jnp.logical_and(has_up, z - t >= 0))
            def _():
                climb(t, j).wait_send()

            @pl.when(jnp.logical_and(has_down, z + t <= planes - 1))
            def _():
                sink(t, j).wait_send()


def gather_plane(planes, normed, wcat, marks):
    rows, width = normed.shape
    _, w_rows, w_cols = wcat.shape
    dma = pltpu.SemaphoreType.DMA
    hops = (planes - 1) * GROUP
    return pl.pallas_call(
        functools.partial(gather_kernel, planes),
        out_shape=(
            jax.ShapeDtypeStruct((GROUP, rows, width), normed.dtype),
            jax.ShapeDtypeStruct((planes * GROUP, w_rows, w_cols), wcat.dtype),
            jax.ShapeDtypeStruct((3, GROUP) + marks.shape, marks.dtype),
        ),
        in_specs=[pl.BlockSpec(memory_space=pltpu.VMEM)] * 3,
        out_specs=(ANY, ANY, ANY),
        scratch_shapes=[
            dma((2 + PIECES,)), dma((PIECES,)), dma((PIECES,)), dma((CHUNKS,)), dma((CHUNKS,)), dma((CHUNKS,)), dma((CHUNKS,)),
            dma((2 * CHUNKS,)), dma((2 * CHUNKS,)), dma((GROUP,)), dma((GROUP,)),
            dma((hops,)), dma((hops,)), dma((hops,)), dma((hops,)), dma((6,)), dma((6,)),
        ],
        compiler_params=pltpu.CompilerParams(
            collective_id=0, has_side_effects=True, vmem_limit_bytes=32 * 1024 * 1024),
        name="gather_plane",
    )(normed, wcat, marks)


def sums_kernel(part_ref, out_ref, slots, send, recv):
    h = lax.axis_index("head")
    s = lax.axis_index("seq")
    g = s % GROUP
    base = s - g
    others = []
    for dh in range(2):
        for d in range(GROUP):
            if (dh, d) != (0, 0):
                others.append((((h + dh) % 2, base + (g + d) % GROUP), dh * GROUP + d))
    greet([(device, None) for device, _ in others])
    mine = h * GROUP + g
    copies = []
    for device, i in others:
        copy = remote(part_ref, slots.at[mine], send.at[i], recv.at[i], device)
        copy.start()
        copies.append(copy)
    slots[mine] = part_ref[...]
    for copy in copies:
        copy.wait()
    total = slots[0]
    for i in range(1, 2 * GROUP):
        total = total + slots[i]
    out_ref[...] = total


def plane_sums(part):
    count = 2 * GROUP
    return pl.pallas_call(
        sums_kernel,
        out_shape=jax.ShapeDtypeStruct(part.shape, part.dtype),
        in_specs=[pl.BlockSpec(memory_space=pltpu.VMEM)],
        out_specs=pl.BlockSpec(memory_space=pltpu.VMEM),
        scratch_shapes=[
            pltpu.VMEM((count,) + part.shape, part.dtype),
            pltpu.SemaphoreType.DMA((count,)),
            pltpu.SemaphoreType.DMA((count,)),
        ],
        compiler_params=pltpu.CompilerParams(collective_id=1, has_side_effects=True),
        name="plane_sums",
    )(part)


def return_kernel(a_ref, o_ref, own, send, recv):
    h = lax.axis_index("head")
    s = lax.axis_index("seq")
    g = s % GROUP
    base = s - g
    width = a_ref.shape[2]
    greet([((h, base + (g + d) % GROUP), None) for d in range(1, GROUP)])
    columns = o_ref.at[:, pl.ds(pl.multiple_of(g * width, 128), width)]
    copies = []
    for d in (2, 3, 1):
        to = (g + d) % GROUP
        copy = remote(a_ref.at[to], columns, send.at[d], recv.at[d], (h, base + to))
        copy.start()
        copies.append(copy)
    here = pltpu.make_async_copy(a_ref.at[g], columns, own)
    here.start()
    here.wait()
    for copy in copies:
        copy.wait()


def return_tokens(attended):
    group, rows, width = attended.shape
    dma = pltpu.SemaphoreType.DMA
    return pl.pallas_call(
        return_kernel,
        out_shape=jax.ShapeDtypeStruct((rows, group * width), attended.dtype),
        in_specs=[ANY],
        out_specs=ANY,
        scratch_shapes=[dma, dma((GROUP,)), dma((GROUP,))],
        compiler_params=pltpu.CompilerParams(collective_id=2, has_side_effects=True),
        name="return_tokens",
    )(attended)


def lanes(x, op):
    out = x[:, :128]
    for i in range(1, BLOCK // 128):
        out = op(out, x[:, i * 128 : (i + 1) * 128])
    return out


def attention_kernel(span_ref, q_ref, k_ref, v_ref, qm_ref, km_ref, o_ref, s_buf):
    block = pl.program_id(0)
    first, last = span_ref[0, block], span_ref[1, block]
    heads = range(q_ref.shape[1] // HEAD_DIM)
    columns = [slice(head * HEAD_DIM, (head + 1) * HEAD_DIM) for head in heads]
    rate = math.log2(math.e) / math.sqrt(HEAD_DIM)
    own = jnp.broadcast_to(qm_ref[...], (BLOCK, BLOCK))

    def rows(b):
        return pl.ds(pl.multiple_of(b * BLOCK, BLOCK), BLOCK)

    def score(b, highest):
        allowed = own == km_ref[b]
        scores = [
            lax.dot_general(
                q_ref[:, columns[head]], k_ref[rows(b), columns[head]], (((1,), (1,)), ((), ())),
                preferred_element_type=jnp.float32)
            for head in heads
        ]
        out = []
        for head in heads:
            s = jnp.where(allowed, scores[head], -1e30)
            s_buf[head, b - first] = s
            out.append(jnp.maximum(highest[head], lanes(s, jnp.maximum)))
        return tuple(out)

    low = jnp.full((BLOCK, 128), -1e30, jnp.float32)
    highest = lax.fori_loop(first, last, score, tuple(low for _ in heads))
    tops = [jnp.max(x, axis=1, keepdims=True) for x in highest]

    def expo(b, totals):
        out = []
        for head in heads:
            e = jnp.exp2((s_buf[head, b - first] - tops[head]) * rate)
            s_buf[head, b - first] = e
            out.append(totals[head] + lanes(e, jnp.add))
        return tuple(out)

    zero = jnp.zeros((BLOCK, 128), jnp.float32)
    totals = lax.fori_loop(first, last, expo, tuple(zero for _ in heads))
    shares = [1.0 / jnp.sum(x, axis=1, keepdims=True) for x in totals]

    def mix(b, accs):
        out = []
        for head in heads:
            w = (s_buf[head, b - first] * shares[head]).astype(jnp.bfloat16)
            out.append(accs[head] + jnp.dot(
                w, v_ref[rows(b), columns[head]], preferred_element_type=jnp.float32))
        return tuple(out)

    accs = lax.fori_loop(first, last, mix, tuple(zero for _ in heads))
    for head in heads:
        o_ref[:, columns[head]] = accs[head].astype(o_ref.dtype)


def attention(q_hat, near_k, near_v, own_marks, near_marks):
    rows, width = q_hat.shape
    near = near_k.shape[0]
    blocks, key_blocks = rows // BLOCK, near // BLOCK
    first_mark = own_marks[::BLOCK]
    last_mark = own_marks[BLOCK - 1 :: BLOCK]
    lowest = jnp.sum((near_marks[None, :] < first_mark[:, None]).astype(jnp.int32), axis=1)
    highest = jnp.sum((near_marks[None, :] <= last_mark[:, None]).astype(jnp.int32), axis=1)
    span = jnp.stack([lowest // BLOCK, (highest + BLOCK - 1) // BLOCK])
    most = min(key_blocks, (BLOCK + 2 * (MOST - 1)) // BLOCK + 1)
    pairs = rows * (BLOCK * 4) * (width // HEAD_DIM)
    return pl.pallas_call(
        attention_kernel,
        grid_spec=pltpu.PrefetchScalarGridSpec(
            num_scalar_prefetch=1,
            grid=(blocks,),
            in_specs=[
                pl.BlockSpec((BLOCK, width), lambda i, span: (i, 0)),
                pl.BlockSpec(memory_space=pltpu.VMEM),
                pl.BlockSpec(memory_space=pltpu.VMEM),
                pl.BlockSpec((BLOCK, 1), lambda i, span: (i, 0)),
                pl.BlockSpec(memory_space=pltpu.VMEM),
            ],
            out_specs=pl.BlockSpec((BLOCK, width), lambda i, span: (i, 0)),
            scratch_shapes=[
                pltpu.VMEM((width // HEAD_DIM, most, BLOCK, BLOCK), jnp.float32),
            ],
        ),
        out_shape=jax.ShapeDtypeStruct((rows, width), jnp.bfloat16),
        compiler_params=pltpu.CompilerParams(vmem_limit_bytes=40 * 1024 * 1024),
        cost_estimate=pl.CostEstimate(
            flops=pairs * HEAD_DIM * 4, bytes_accessed=near * width * 4 + rows * width * 4,
            transcendentals=pairs),
        name="tile_attention",
    )(span, q_hat, near_k, near_v, own_marks[:, None], near_marks.reshape(key_blocks, 1, BLOCK))


def norm_kernel(t_ref, gain_ref, o_ref):
    floats = t_ref[...].astype(jnp.float32)
    square = jnp.mean(floats * floats, axis=1, keepdims=True)
    o_ref[...] = (floats * lax.rsqrt(square + EPS) * gain_ref[...]).astype(o_ref.dtype)


def norm_tokens(tokens, gain):
    rows, width = tokens.shape
    part = 128
    return pl.pallas_call(
        norm_kernel,
        grid=(rows // part,),
        in_specs=[
            pl.BlockSpec((part, width), lambda i: (i, 0)),
            pl.BlockSpec((1, width), lambda i: (0, 0)),
        ],
        out_specs=pl.BlockSpec((part, width), lambda i: (i, 0)),
        out_shape=jax.ShapeDtypeStruct((rows, width), jnp.bfloat16),
        compiler_params=pltpu.CompilerParams(vmem_limit_bytes=32 * 1024 * 1024),
        cost_estimate=pl.CostEstimate(
            flops=rows * width * 4, bytes_accessed=rows * width * 4, transcendentals=rows),
        name="norm_tokens",
    )(tokens, gain[None, :])


def from_behind(shard, by):
    size = lax.axis_size("seq")
    pairs = [(i, i + by) for i in range(size) if 0 <= i + by < size]
    return lax.ppermute(shard, "seq", pairs)


def with_halo(shard, step):
    rows_here = shard.shape[0]
    left, right, need, distance = [], [], MOST - 1, 1
    while need > 0:
        take = min(need, rows_here)
        left.insert(0, from_behind(shard[rows_here - take :], distance * step))
        right.append(from_behind(shard[:take], -distance * step))
        need, distance = need - take, distance + 1
    return jnp.concatenate(left + [shard] + right, axis=0)


def on_device(grouped, tokens, ln_gain, w_query, w_key, w_value, q_gain, k_gain, seg_ids):
    heads_here = w_query.shape[1] // HEAD_DIM
    total_channels = HEADS * HEAD_DIM
    place = lax.axis_index("seq")
    seq = lax.axis_size("seq")
    margin = MOST - 1
    normed = norm_tokens(tokens, ln_gain)
    low, high = -1, jnp.iinfo(jnp.int32).max
    if grouped:
        share = w_query.shape[1] // GROUP
        step = GROUP
        member = place % GROUP
        wcat = jnp.concatenate(
            [w.reshape(w.shape[0], GROUP, share) for w in (w_key, w_value, w_query)], axis=2
        ).transpose(1, 0, 2)
        near_tokens, weights, marks = gather_plane(
            seq // GROUP, normed, wcat, seg_ids.reshape(-1, 128)
        )
        plane = place // GROUP
        marks = marks.reshape(3, -1)
        own_marks = marks[1]
        left = jnp.where(plane > 0, marks[0, marks.shape[1] - margin :], low)
        right = jnp.where(plane < seq // GROUP - 1, marks[2, :margin], high)
        near_marks = jnp.concatenate([left, own_marks, right])
        rows = GROUP * tokens.shape[0]
        near_tokens = near_tokens.reshape(rows, tokens.shape[1])
        weights = weights.reshape(tokens.shape[1], 3 * share)
        q_gain = lax.dynamic_slice_in_dim(q_gain, member * share, share)
        k_gain = lax.dynamic_slice_in_dim(k_gain, member * share, share)
    else:
        step = 1
        rows = tokens.shape[0]
        near_tokens = normed
        share = w_query.shape[1]
        weights = jnp.concatenate([w_key, w_value, w_query], axis=1)
        weights = lax.all_gather(weights, "seq", axis=0, tiled=True)
        all_marks = lax.all_gather(seg_ids, "seq", axis=0, tiled=True)
        padded = jnp.concatenate(
            [jnp.full((margin,), low, jnp.int32), all_marks, jnp.full((margin,), high, jnp.int32)]
        )
        near_marks = lax.dynamic_slice_in_dim(padded, place * rows, rows + 2 * margin)
        own_marks = seg_ids

    def project(w):
        return jnp.dot(near_tokens, w, preferred_element_type=jnp.float32)

    def norm(part, gain):
        square = jnp.sum(part * part, axis=1)
        if grouped:
            square = plane_sums(square.reshape(rows // 128, 128)).reshape(rows)
        else:
            square = lax.psum(square, "head")
        return (part * lax.rsqrt(square[:, None] / total_channels + EPS) * gain).astype(jnp.bfloat16)

    both = project(weights[:, : 2 * share])
    near_v = with_halo(both[:, share:].astype(jnp.bfloat16), step)
    near_k = with_halo(norm(both[:, :share], k_gain), step)
    q_hat = norm(project(weights[:, 2 * share :]), q_gain)
    attended = attention(q_hat, near_k, near_v, own_marks, near_marks)
    if grouped:
        attended = return_tokens(attended.reshape(GROUP, tokens.shape[0], attended.shape[1]))
    return attended


def solution(mesh):
    seq, heads = mesh.shape["seq"], mesh.shape["head"]
    grouped = heads == 2 and seq % GROUP == 0 and HEADS // heads % GROUP == 0
    return jax.shard_map(
        functools.partial(on_device, grouped),
        mesh=mesh,
        in_specs=(
            P("seq", None),
            P(),
            P("seq", "head"),
            P("seq", "head"),
            P("seq", "head"),
            P("head"),
            P("head"),
            P("seq"),
        ),
        out_specs=P("seq", "head"),
        check_vma=False,
    )
```

```python
import functools
import math

import jax
import jax.numpy as jnp
from jax import lax
from jax.experimental import pallas as pl
from jax.experimental.pallas import tpu as pltpu
from jax.sharding import PartitionSpec as P

HEADS = 16
HEAD_DIM = 128
MOST = 1025
EPS = 1e-06
GROUP = 4
CHUNKS = 4
PIECES = 8
BLOCK = 256
MESH = pl.DeviceIdType.MESH
ANY = pl.BlockSpec(memory_space=pl.ANY)


def greet(partners):
    barrier = pltpu.get_barrier_semaphore()
    count = 0
    for device, there in partners:
        if there is None:
            pl.semaphore_signal(barrier, inc=1, device_id=device, device_id_type=MESH)
            count = count + 1
        else:

            @pl.when(there)
            def _(device=device):
                pl.semaphore_signal(barrier, inc=1, device_id=device, device_id_type=MESH)

            count = count + there.astype(jnp.int32)
    pl.semaphore_wait(barrier, count)


def remote(src, dst, send, recv, device):
    return pltpu.make_async_remote_copy(
        src_ref=src, dst_ref=dst, send_sem=send, recv_sem=recv,
        device_id=device, device_id_type=MESH,
    )


def gather_kernel(planes, n_ref, w_ref, m_ref, x_out, w_out, m_out, own_sem, core_s, core_r, y_s, y_r, x_s, x_r,
                  cf_s, cf_r, a_s, a_r, up_s, up_r, down_s, down_r, mark_s, mark_r):
    h = lax.axis_index("head")
    s = lax.axis_index("seq")
    z, g = s // GROUP, s % GROUP
    y, c = g // 2, g % 2
    base = z * GROUP
    core_g = y * 2 + (1 - c)
    far_g = (1 - y) * 2 + c
    core_dev, y_dev, x_dev = (h, base + core_g), (h, base + far_g), (1 - h, s)
    up_dev = (h, jnp.minimum(s + GROUP, planes * GROUP - 1))
    down_dev = (h, jnp.maximum(s - GROUP, 0))
    has_up, has_down = z < planes - 1, z > 0
    member = [(y + d // 2) % 2 * 2 + (c + d % 2) % 2 for d in range(GROUP)]
    group_dev = [(h, base + m) for m in member]
    greet([(x_dev, None)] + [(group_dev[d], None) for d in range(1, GROUP)]
          + [(up_dev, has_up), (down_dev, has_down)])

    rows = n_ref.shape[0]
    half = rows // 2
    piece = half // CHUNKS

    def spread(d):
        return remote(w_ref.at[member[d]], w_out.at[s], a_s.at[d], a_r.at[d], group_dev[d])

    def climb(t, j):
        slot = (z - t) * GROUP + member[j]
        src = w_ref.at[g] if (t, j) == (0, 0) else w_out.at[slot]
        return remote(src, w_out.at[slot], up_s.at[t * GROUP + j], up_r.at[t * GROUP + j], up_dev)

    def sink(t, j):
        slot = (z + t) * GROUP + member[j]
        src = w_ref.at[g] if (t, j) == (0, 0) else w_out.at[slot]
        return remote(src, w_out.at[slot], down_s.at[t * GROUP + j], down_r.at[t * GROUP + j], down_dev)

    def any_slot(sem_s, sem_r, device):
        return remote(w_out.at[0], w_out.at[0], sem_s, sem_r, device)

    def token_rows(block, which, k):
        return x_out.at[block, pl.ds(pl.multiple_of(which * half + k * piece, 16), piece)]

    def over_y(k):
        first = pl.multiple_of(h * half + k * piece, 16)
        return remote(n_ref.at[pl.ds(first, piece)], token_rows(g, h, k), y_s.at[k], y_r.at[k], y_dev)

    def over_x(k):
        part = token_rows(far_g, h, k)
        return remote(part, part, x_s.at[k], x_r.at[k], x_dev)

    def over_core(k, from_x):
        part = token_rows(far_g, 1 - h if from_x else h, k)
        i = CHUNKS + k if from_x else k
        return remote(part, part, cf_s.at[i], cf_r.at[i], core_dev)

    own_w = pltpu.make_async_copy(w_ref.at[g], w_out.at[s], own_sem.at[0])
    slab = rows // PIECES

    def own_x(i):
        part = pl.ds(i * slab, slab)
        return pltpu.make_async_copy(n_ref.at[part], x_out.at[g, part], own_sem.at[2 + i])

    def block_core(i):
        part = pl.ds(i * slab, slab)
        return remote(n_ref.at[part], x_out.at[g, part], core_s.at[i], core_r.at[i], core_dev)

    own_m = pltpu.make_async_copy(m_ref, m_out.at[1, g], own_sem.at[1])

    def spread_marks(d):
        return remote(m_ref, m_out.at[1, g], mark_s.at[d], mark_r.at[d], group_dev[d])

    marks_up = remote(m_out.at[1], m_out.at[0], mark_s.at[4], mark_r.at[4], up_dev)
    marks_down = remote(m_out.at[1], m_out.at[2], mark_s.at[5], mark_r.at[5], down_dev)

    def send_z(t, j):
        @pl.when(jnp.logical_and(has_up, z - t >= 0))
        def _():
            climb(t, j).start()

        @pl.when(jnp.logical_and(has_down, z + t <= planes - 1))
        def _():
            sink(t, j).start()

    def take_z(t, j):
        i = t * GROUP + j

        @pl.when(z - 1 - t >= 0)
        def _():
            any_slot(up_s.at[i], up_r.at[i], down_dev).wait_recv()

        @pl.when(z + 1 + t <= planes - 1)
        def _():
            any_slot(down_s.at[i], down_r.at[i], up_dev).wait_recv()

        if t + 1 <= planes - 2:
            send_z(t + 1, j)

    own_m.start()
    send_z(0, 0)
    for d in (1, 2, 3):
        spread(d).start()
        spread_marks(d).start()
    over_y(0).start()
    over_y(1).start()
    over_y(2).start()
    own_w.start()
    for i in range(PIECES):
        block_core(i).start()
        own_x(i).start()

    def take_y(k):
        over_y(k).wait_recv()
        over_x(k).start()
        over_core(k, False).start()
        if k + 3 < CHUNKS:
            over_y(k + 3).start()

    def take_x(k):
        over_x(k).wait_recv()
        over_core(k, True).start()

    def take_spread(d):
        spread(d).wait_recv()
        send_z(0, d)

    take_spread(1)
    take_z(0, 0)
    take_spread(2)
    take_spread(3)
    take_z(0, 1)
    own_m.wait()
    for d in range(1, GROUP):
        spread_marks(d).wait_recv()

    @pl.when(has_up)
    def _():
        marks_up.start()

    @pl.when(has_down)
    def _():
        marks_down.start()

    take_z(0, 2)
    take_y(0)
    hops = [(0, 3)] + [(t, j) for t in range(1, planes - 1) for j in range(GROUP)]
    moves = [(take_y, k) for k in range(1, CHUNKS)] + [(take_x, k) for k in range(CHUNKS)]
    moves.sort(key=lambda move: move[1] + (0.5 if move[0] is take_x else -0.5))
    done = 0
    for i, hop in enumerate(hops):
        take_z(*hop)
        until = min(len(moves), (i * len(moves) + len(hops) - 1) // max(len(hops) - 1, 1))
        for move, k in moves[done:until]:
            move(k)
        done = max(done, until)
    for move, k in moves[done:]:
        move(k)

    own_w.wait()
    for i in range(PIECES):
        own_x(i).wait()
        block_core(i).wait()
    for k in range(CHUNKS):
        over_y(k).wait_send()
        over_x(k).wait_send()
        over_core(k, False).wait()
        over_core(k, True).wait()
    for d in range(1, GROUP):
        spread(d).wait_send()
        spread_marks(d).wait_send()

    @pl.when(has_up)
    def _():
        marks_up.wait_send()
        marks_down.wait_recv()

    @pl.when(has_down)
    def _():
        marks_down.wait_send()
        marks_up.wait_recv()

    for t in range(planes - 1):
        for j in range(GROUP):

            @pl.when(jnp.logical_and(has_up, z - t >= 0))
            def _():
                climb(t, j).wait_send()

            @pl.when(jnp.logical_and(has_down, z + t <= planes - 1))
            def _():
                sink(t, j).wait_send()


def gather_plane(planes, normed, wcat, marks):
    rows, width = normed.shape
    _, w_rows, w_cols = wcat.shape
    dma = pltpu.SemaphoreType.DMA
    hops = (planes - 1) * GROUP
    return pl.pallas_call(
        functools.partial(gather_kernel, planes),
        out_shape=(
            jax.ShapeDtypeStruct((GROUP, rows, width), normed.dtype),
            jax.ShapeDtypeStruct((planes * GROUP, w_rows, w_cols), wcat.dtype),
            jax.ShapeDtypeStruct((3, GROUP) + marks.shape, marks.dtype),
        ),
        in_specs=[pl.BlockSpec(memory_space=pltpu.VMEM)] * 3,
        out_specs=(ANY, ANY, ANY),
        scratch_shapes=[
            dma((2 + PIECES,)), dma((PIECES,)), dma((PIECES,)), dma((CHUNKS,)), dma((CHUNKS,)), dma((CHUNKS,)), dma((CHUNKS,)),
            dma((2 * CHUNKS,)), dma((2 * CHUNKS,)), dma((GROUP,)), dma((GROUP,)),
            dma((hops,)), dma((hops,)), dma((hops,)), dma((hops,)), dma((6,)), dma((6,)),
        ],
        compiler_params=pltpu.CompilerParams(
            collective_id=0, has_side_effects=True, vmem_limit_bytes=32 * 1024 * 1024),
        name="gather_plane",
    )(normed, wcat, marks)


def sums_kernel(part_ref, out_ref, slots, send, recv):
    h = lax.axis_index("head")
    s = lax.axis_index("seq")
    g = s % GROUP
    base = s - g
    others = []
    for dh in range(2):
        for d in range(GROUP):
            if (dh, d) != (0, 0):
                others.append((((h + dh) % 2, base + (g + d) % GROUP), dh * GROUP + d))
    greet([(device, None) for device, _ in others])
    mine = h * GROUP + g
    copies = []
    for device, i in others:
        copy = remote(part_ref, slots.at[mine], send.at[i], recv.at[i], device)
        copy.start()
        copies.append(copy)
    slots[mine] = part_ref[...]
    for copy in copies:
        copy.wait()
    total = slots[0]
    for i in range(1, 2 * GROUP):
        total = total + slots[i]
    out_ref[...] = total


def plane_sums(part):
    count = 2 * GROUP
    return pl.pallas_call(
        sums_kernel,
        out_shape=jax.ShapeDtypeStruct(part.shape, part.dtype),
        in_specs=[pl.BlockSpec(memory_space=pltpu.VMEM)],
        out_specs=pl.BlockSpec(memory_space=pltpu.VMEM),
        scratch_shapes=[
            pltpu.VMEM((count,) + part.shape, part.dtype),
            pltpu.SemaphoreType.DMA((count,)),
            pltpu.SemaphoreType.DMA((count,)),
        ],
        compiler_params=pltpu.CompilerParams(collective_id=1, has_side_effects=True),
        name="plane_sums",
    )(part)


def return_kernel(a_ref, o_ref, own, send, recv):
    h = lax.axis_index("head")
    s = lax.axis_index("seq")
    g = s % GROUP
    base = s - g
    width = a_ref.shape[2]
    greet([((h, base + (g + d) % GROUP), None) for d in range(1, GROUP)])
    columns = o_ref.at[:, pl.ds(pl.multiple_of(g * width, 128), width)]
    copies = []
    for d in (2, 3, 1):
        to = (g + d) % GROUP
        copy = remote(a_ref.at[to], columns, send.at[d], recv.at[d], (h, base + to))
        copy.start()
        copies.append(copy)
    here = pltpu.make_async_copy(a_ref.at[g], columns, own)
    here.start()
    here.wait()
    for copy in copies:
        copy.wait()


def return_tokens(attended):
    group, rows, width = attended.shape
    dma = pltpu.SemaphoreType.DMA
    return pl.pallas_call(
        return_kernel,
        out_shape=jax.ShapeDtypeStruct((rows, group * width), attended.dtype),
        in_specs=[pl.BlockSpec(memory_space=pltpu.VMEM)],
        out_specs=ANY,
        scratch_shapes=[dma, dma((GROUP,)), dma((GROUP,))],
        compiler_params=pltpu.CompilerParams(collective_id=2, has_side_effects=True),
        name="return_tokens",
    )(attended)


def lanes(x, op):
    out = x[:, :128]
    for i in range(1, BLOCK // 128):
        out = op(out, x[:, i * 128 : (i + 1) * 128])
    return out


def attention_kernel(span_ref, q_ref, k_ref, v_ref, qm_ref, km_ref, o_ref, s_buf):
    block = pl.program_id(0)
    first, last = span_ref[0, block], span_ref[1, block]
    heads = range(q_ref.shape[1] // HEAD_DIM)
    columns = [slice(head * HEAD_DIM, (head + 1) * HEAD_DIM) for head in heads]
    rate = math.log2(math.e) / math.sqrt(HEAD_DIM)
    own = jnp.broadcast_to(qm_ref[...], (BLOCK, BLOCK))

    def rows(b):
        return pl.ds(pl.multiple_of(b * BLOCK, BLOCK), BLOCK)

    def score(b, highest):
        allowed = own == km_ref[b]
        scores = [
            lax.dot_general(
                q_ref[:, columns[head]], k_ref[rows(b), columns[head]], (((1,), (1,)), ((), ())),
                preferred_element_type=jnp.float32)
            for head in heads
        ]
        out = []
        for head in heads:
            s = jnp.where(allowed, scores[head], -1e30)
            s_buf[head, b - first] = s
            out.append(jnp.maximum(highest[head], lanes(s, jnp.maximum)))
        return tuple(out)

    low = jnp.full((BLOCK, 128), -1e30, jnp.float32)
    highest = lax.fori_loop(first, last, score, tuple(low for _ in heads))
    tops = [jnp.max(x, axis=1, keepdims=True) for x in highest]

    def expo(b, totals):
        out = []
        for head in heads:
            e = jnp.exp2((s_buf[head, b - first] - tops[head]) * rate)
            s_buf[head, b - first] = e
            out.append(totals[head] + lanes(e, jnp.add))
        return tuple(out)

    zero = jnp.zeros((BLOCK, 128), jnp.float32)
    totals = lax.fori_loop(first, last, expo, tuple(zero for _ in heads))
    shares = [1.0 / jnp.sum(x, axis=1, keepdims=True) for x in totals]

    def mix(b, accs):
        out = []
        for head in heads:
            w = (s_buf[head, b - first] * shares[head]).astype(jnp.bfloat16)
            out.append(accs[head] + jnp.dot(
                w, v_ref[rows(b), columns[head]], preferred_element_type=jnp.float32))
        return tuple(out)

    accs = lax.fori_loop(first, last, mix, tuple(zero for _ in heads))
    for head in heads:
        o_ref[:, columns[head]] = accs[head].astype(o_ref.dtype)


def attention(q_hat, near_k, near_v, own_marks, near_marks):
    rows, width = q_hat.shape
    near = near_k.shape[0]
    blocks, key_blocks = rows // BLOCK, near // BLOCK
    first_mark = own_marks[::BLOCK]
    last_mark = own_marks[BLOCK - 1 :: BLOCK]
    lowest = jnp.sum((near_marks[None, :] < first_mark[:, None]).astype(jnp.int32), axis=1)
    highest = jnp.sum((near_marks[None, :] <= last_mark[:, None]).astype(jnp.int32), axis=1)
    span = jnp.stack([lowest // BLOCK, (highest + BLOCK - 1) // BLOCK])
    most = min(key_blocks, (BLOCK + 2 * (MOST - 1)) // BLOCK + 1)
    pairs = rows * (BLOCK * 4) * (width // HEAD_DIM)
    return pl.pallas_call(
        attention_kernel,
        grid_spec=pltpu.PrefetchScalarGridSpec(
            num_scalar_prefetch=1,
            grid=(blocks,),
            in_specs=[
                pl.BlockSpec((BLOCK, width), lambda i, span: (i, 0)),
                pl.BlockSpec(memory_space=pltpu.VMEM),
                pl.BlockSpec(memory_space=pltpu.VMEM),
                pl.BlockSpec((BLOCK, 1), lambda i, span: (i, 0)),
                pl.BlockSpec(memory_space=pltpu.VMEM),
            ],
            out_specs=pl.BlockSpec((BLOCK, width), lambda i, span: (i, 0)),
            scratch_shapes=[
                pltpu.VMEM((width // HEAD_DIM, most, BLOCK, BLOCK), jnp.float32),
            ],
        ),
        out_shape=jax.ShapeDtypeStruct((rows, width), jnp.bfloat16),
        compiler_params=pltpu.CompilerParams(vmem_limit_bytes=40 * 1024 * 1024),
        cost_estimate=pl.CostEstimate(
            flops=pairs * HEAD_DIM * 4, bytes_accessed=near * width * 4 + rows * width * 4,
            transcendentals=pairs),
        name="tile_attention",
    )(span, q_hat, near_k, near_v, own_marks[:, None], near_marks.reshape(key_blocks, 1, BLOCK))


def norm_kernel(t_ref, gain_ref, o_ref):
    floats = t_ref[...].astype(jnp.float32)
    square = jnp.mean(floats * floats, axis=1, keepdims=True)
    o_ref[...] = (floats * lax.rsqrt(square + EPS) * gain_ref[...]).astype(o_ref.dtype)


def norm_tokens(tokens, gain):
    rows, width = tokens.shape
    part = 128
    return pl.pallas_call(
        norm_kernel,
        grid=(rows // part,),
        in_specs=[
            pl.BlockSpec((part, width), lambda i: (i, 0)),
            pl.BlockSpec((1, width), lambda i: (0, 0)),
        ],
        out_specs=pl.BlockSpec((part, width), lambda i: (i, 0)),
        out_shape=jax.ShapeDtypeStruct((rows, width), jnp.bfloat16),
        compiler_params=pltpu.CompilerParams(vmem_limit_bytes=32 * 1024 * 1024),
        cost_estimate=pl.CostEstimate(
            flops=rows * width * 4, bytes_accessed=rows * width * 4, transcendentals=rows),
        name="norm_tokens",
    )(tokens, gain[None, :])


def project_kernel(x_ref, w_ref, *o_refs):
    part = jnp.dot(x_ref[...], w_ref[...], preferred_element_type=jnp.float32)
    width = o_refs[0].shape[1]
    for i, o_ref in enumerate(o_refs):
        o_ref[...] = part[:, i * width : (i + 1) * width].astype(o_ref.dtype)


def project(x, weights, width, place, kinds):
    rows, depth = x.shape
    cols = width * len(kinds)
    return pl.pallas_call(
        project_kernel,
        grid=(rows // BLOCK,),
        in_specs=[
            pl.BlockSpec((BLOCK, depth), lambda i: (i, 0)),
            pl.BlockSpec((depth, cols), lambda i: (0, place)),
        ],
        out_specs=tuple(pl.BlockSpec((BLOCK, width), lambda i: (i, 0)) for _ in kinds),
        out_shape=tuple(jax.ShapeDtypeStruct((rows, width), kind) for kind in kinds),
        compiler_params=pltpu.CompilerParams(vmem_limit_bytes=40 * 1024 * 1024),
        cost_estimate=pl.CostEstimate(
            flops=2 * rows * depth * cols, bytes_accessed=2 * depth * (rows + cols) + 4 * rows * cols,
            transcendentals=0),
        name="project",
    )(x, weights)


def from_behind(shard, by):
    size = lax.axis_size("seq")
    pairs = [(i, i + by) for i in range(size) if 0 <= i + by < size]
    return lax.ppermute(shard, "seq", pairs)


def with_halo(shard, step):
    rows_here = shard.shape[0]
    left, right, need, distance = [], [], MOST - 1, 1
    while need > 0:
        take = min(need, rows_here)
        left.insert(0, from_behind(shard[rows_here - take :], distance * step))
        right.append(from_behind(shard[:take], -distance * step))
        need, distance = need - take, distance + 1
    return jnp.concatenate(left + [shard] + right, axis=0)


def on_device(grouped, tokens, ln_gain, w_query, w_key, w_value, q_gain, k_gain, seg_ids):
    heads_here = w_query.shape[1] // HEAD_DIM
    total_channels = HEADS * HEAD_DIM
    place = lax.axis_index("seq")
    seq = lax.axis_size("seq")
    margin = MOST - 1
    normed = norm_tokens(tokens, ln_gain)
    low, high = -1, jnp.iinfo(jnp.int32).max
    if grouped:
        share = w_query.shape[1] // GROUP
        step = GROUP
        member = place % GROUP
        wcat = jnp.concatenate(
            [w.reshape(w.shape[0], GROUP, share) for w in (w_key, w_value, w_query)], axis=2
        ).transpose(1, 0, 2)
        near_tokens, weights, marks = gather_plane(
            seq // GROUP, normed, wcat, seg_ids.reshape(-1, 128)
        )
        plane = place // GROUP
        marks = marks.reshape(3, -1)
        own_marks = marks[1]
        left = jnp.where(plane > 0, marks[0, marks.shape[1] - margin :], low)
        right = jnp.where(plane < seq // GROUP - 1, marks[2, :margin], high)
        near_marks = jnp.concatenate([left, own_marks, right])
        rows = GROUP * tokens.shape[0]
        near_tokens = near_tokens.reshape(rows, tokens.shape[1])
        weights = weights.reshape(tokens.shape[1], 3 * share)
        q_gain = lax.dynamic_slice_in_dim(q_gain, member * share, share)
        k_gain = lax.dynamic_slice_in_dim(k_gain, member * share, share)
    else:
        step = 1
        rows = tokens.shape[0]
        near_tokens = normed
        share = w_query.shape[1]
        weights = jnp.concatenate([w_key, w_value, w_query], axis=1)
        weights = lax.all_gather(weights, "seq", axis=0, tiled=True)
        all_marks = lax.all_gather(seg_ids, "seq", axis=0, tiled=True)
        padded = jnp.concatenate(
            [jnp.full((margin,), low, jnp.int32), all_marks, jnp.full((margin,), high, jnp.int32)]
        )
        near_marks = lax.dynamic_slice_in_dim(padded, place * rows, rows + 2 * margin)
        own_marks = seg_ids

    def norm(part, gain):
        square = jnp.sum(part * part, axis=1)
        if grouped:
            square = plane_sums(square.reshape(rows // 128, 128)).reshape(rows)
        else:
            square = lax.psum(square, "head")
        return (part * lax.rsqrt(square[:, None] / total_channels + EPS) * gain).astype(jnp.bfloat16)

    key_part, v_hat = project(near_tokens, weights, share, 0, (jnp.float32, jnp.bfloat16))
    near_v = with_halo(v_hat, step)
    near_k = with_halo(norm(key_part, k_gain), step)
    (queries,) = project(near_tokens, weights, share, 2, (jnp.float32,))
    q_hat = norm(queries, q_gain)
    attended = attention(q_hat, near_k, near_v, own_marks, near_marks)
    if grouped:
        attended = return_tokens(attended.reshape(GROUP, tokens.shape[0], attended.shape[1]))
    return attended


def solution(mesh):
    seq, heads = mesh.shape["seq"], mesh.shape["head"]
    grouped = heads == 2 and seq % GROUP == 0 and HEADS // heads % GROUP == 0
    return jax.shard_map(
        functools.partial(on_device, grouped),
        mesh=mesh,
        in_specs=(
            P("seq", None),
            P(),
            P("seq", "head"),
            P("seq", "head"),
            P("seq", "head"),
            P("head"),
            P("head"),
            P("seq"),
        ),
        out_specs=P("seq", "head"),
        check_vma=False,
    )
```
